32 devices in a mesh: dp: 8 (over z, x), mp: 4 (over y, core).
Axes of the slice: x: 2, y: 2, z: 4, core: 2. Of those that a mesh axis runs over, the one named last changes fastest.
Arguments:
- queries: bfloat16 [128, 80, 8192], P('dp', None, 'mp'), may hold values from -1.5 to 1.5
- response_keys: bfloat16 [128, 80, 1024], P('dp', None, 'mp'), may hold values from -1.5 to 1.5
- response_values: bfloat16 [128, 80, 1024], P('dp', None, 'mp'), may hold values from -6 to 6
- output_gradient: bfloat16 [128, 80, 8192], P('dp', None, 'mp'), may hold values from -16 to 16
- prompt_token_keys: bfloat16 [8, 256, 1024], P('dp', None, 'mp'), may hold values from -1.5 to 1.5
- prompt_token_values: bfloat16 [8, 256, 1024], P('dp', None, 'mp'), may hold values from -6 to 6
- normed_hidden_input: bfloat16 [128, 80, 5120], P('dp', None, 'mp'), may hold values from -6 to 6
- adapter_down_factor: bfloat16 [5120, 32], P('mp'), may hold values from -0.078125 to 0.078125
- adapter_up_factor: bfloat16 [32, 8192], P(None, 'mp'), may hold values from -0.0625 to 0.0625
- response_prompt_index: int32 [128], P('dp'), may hold values from 0 to 7, as said below
- response_lengths: int32 [128], P('dp'), may hold values from 1 to 80, as said below
Outputs:
- query_grad: bfloat16 [128, 80, 8192], P('dp', None, 'mp')
- response_key_gradient: bfloat16 [128, 80, 1024], P('dp', None, 'mp')
- response_value_gradient: bfloat16 [128, 80, 1024], P('dp', None, 'mp')
- prompt_key_grad: bfloat16 [8, 256, 1024], P('dp', None, 'mp')
- prompt_value_grad: bfloat16 [8, 256, 1024], P('dp', None, 'mp')
- down_factor_gradient: float32 [5120, 32], P('mp')
- up_factor_gradient: float32 [32, 8192], P(None, 'mp')
The draws below stay inside these ranges and needn't reach their ends.
Inputs may be any that keep to these rules, and one draw needn't show every extreme that they name: `response_prompt_index`: responses 16 * d to 16 * d + 15 are those held by index d of dp, and prompt p is held by index p. Every prompt is named by exactly 16 responses; the responses of one index of dp come from exactly 4 prompts, 4 from each. `response_lengths`: among the 16 responses of each index of dp at least one has length 80.
All inputs are finite; a program needn't handle non-finite values.
Results may differ from the reference program's by a relative error of at most 0.017.
Values may be sent and summed in bfloat16 or wider, within the bound.
A program may use at most 128 MiB of HBM per device.

```python
import math
import jax
import jax.numpy as jnp
from jax import lax

MODEL_WIDTH = 5120
QUERY_HEAD_COUNT = 64
KEY_VALUE_HEADS = 8
HEAD_SIZE = 128
ADAPTER_RANK = 32
GROUP = 16
SHARE = 4
RESPONSE_LENGTH = 80
PROMPT_LENGTH = 256
PROMPT_COUNT = 8
RESPONSE_COUNT = 128
TOTAL_TOKENS = 10240
N_DP = 8


def draw_response_prompt_index(key, part):
    key = jax.random.fold_in(key, 11)
    first, second, third = jax.random.split(key, 3)
    holders = jax.random.permutation(first, PROMPT_COUNT)
    blocks = GROUP // SHARE
    offsets = jax.random.permutation(second, PROMPT_COUNT)[:blocks]
    device_ids = jnp.arange(PROMPT_COUNT, dtype=jnp.int32)[:, None]
    chosen = holders[(device_ids + offsets[None, :]) % PROMPT_COUNT]
    slots = jnp.repeat(chosen, SHARE, axis=1)
    device_keys = jax.random.split(third, PROMPT_COUNT)
    orders = jax.vmap(lambda one_key: jax.random.permutation(one_key, GROUP))(device_keys)
    slots = jnp.take_along_axis(slots, orders, axis=1)
    return slots.reshape(RESPONSE_COUNT).astype(jnp.int32)


def draw_response_lengths(key, part):
    key = jax.random.fold_in(key, 23)
    first, second = jax.random.split(key)
    lengths = jax.random.randint(first, (PROMPT_COUNT, GROUP), 1, RESPONSE_LENGTH + 1)
    longest = jax.random.randint(second, (PROMPT_COUNT,), 0, GROUP)
    lengths = jnp.where(jnp.arange(GROUP)[None, :] == longest[:, None], RESPONSE_LENGTH, lengths)
    return lengths.reshape(RESPONSE_COUNT).astype(jnp.int32)


def block_levels(rng, extent, cuts, low, largest):
    def one(axis_at, parts):
        steps = jax.random.uniform(jax.random.fold_in(jax.random.fold_in(rng, 6), axis_at), (parts,), jnp.float32, low / len(cuts), largest / len(cuts))
        return jnp.repeat(jnp.exp(steps), extent[axis_at] // parts).reshape((-1,) + (1,) * (len(extent) - axis_at - 1))

    level = one(*cuts[0])
    for cut in cuts[1:]:
        level = level * one(*cut)
    return level


def bell_draw(rng, shape, deviation, limit, cuts=(), held_as=jnp.bfloat16):
    factor_of = block_levels(rng, shape, cuts, -0.22, 0.18) if cuts else 1.0
    values = jax.random.normal(rng, shape, jnp.float32) * deviation * factor_of
    return jnp.minimum(jnp.maximum(values, -limit), limit).astype(held_as)


def setup_inputs(seed: int = 0) -> dict:
    seeds = jax.random.split(jax.random.key(seed), 12)
    queries = jnp.clip(jax.random.uniform(seeds[0], (RESPONSE_COUNT, RESPONSE_LENGTH, QUERY_HEAD_COUNT * HEAD_SIZE), jnp.float32, -1.5, 1.5) * block_levels(seeds[0], (RESPONSE_COUNT, RESPONSE_LENGTH, QUERY_HEAD_COUNT * HEAD_SIZE), ((0, 8), (2, 4)), -0.4, 0.0), -1.5, 1.5).astype(jnp.bfloat16)
    response_keys = jnp.clip(jax.random.uniform(seeds[1], (RESPONSE_COUNT, RESPONSE_LENGTH, KEY_VALUE_HEADS * HEAD_SIZE), jnp.float32, -1.5, 1.5) * block_levels(seeds[1], (RESPONSE_COUNT, RESPONSE_LENGTH, KEY_VALUE_HEADS * HEAD_SIZE), ((0, 8), (2, 4)), -0.4, 0.0), -1.5, 1.5).astype(jnp.bfloat16)
    response_values = bell_draw(seeds[2], (RESPONSE_COUNT, RESPONSE_LENGTH, KEY_VALUE_HEADS * HEAD_SIZE), 1.0, 6.0, ((0, 8), (2, 4)))
    output_gradient = jnp.clip(jax.random.uniform(seeds[3], (RESPONSE_COUNT, RESPONSE_LENGTH, QUERY_HEAD_COUNT * HEAD_SIZE), jnp.float32, -16.0, 16.0) * block_levels(seeds[3], (RESPONSE_COUNT, RESPONSE_LENGTH, QUERY_HEAD_COUNT * HEAD_SIZE), ((0, 8), (2, 4)), -0.4, 0.0), -16.0, 16.0).astype(jnp.bfloat16)
    prompt_token_keys = jnp.clip(jax.random.uniform(seeds[4], (PROMPT_COUNT, PROMPT_LENGTH, KEY_VALUE_HEADS * HEAD_SIZE), jnp.float32, -1.5, 1.5) * block_levels(seeds[4], (PROMPT_COUNT, PROMPT_LENGTH, KEY_VALUE_HEADS * HEAD_SIZE), ((0, 8), (2, 4)), -0.4, 0.0), -1.5, 1.5).astype(jnp.bfloat16)
    prompt_token_values = bell_draw(seeds[5], (PROMPT_COUNT, PROMPT_LENGTH, KEY_VALUE_HEADS * HEAD_SIZE), 1.0, 6.0, ((0, 8), (2, 4)))
    normed_hidden_input = bell_draw(seeds[6], (RESPONSE_COUNT, RESPONSE_LENGTH, MODEL_WIDTH), 1.0, 6.0, ((0, 8), (2, 4)))
    adapter_down_factor = bell_draw(seeds[7], (MODEL_WIDTH, ADAPTER_RANK), MODEL_WIDTH ** -0.5, 0.078125, ((0, 4),))
    adapter_up_factor = bell_draw(seeds[8], (ADAPTER_RANK, QUERY_HEAD_COUNT * HEAD_SIZE), (QUERY_HEAD_COUNT * HEAD_SIZE) ** -0.5, 0.0625, ((1, 4),))
    response_prompt_index = draw_response_prompt_index(jax.random.fold_in(seeds[11], 71), 0)
    response_lengths = draw_response_lengths(jax.random.fold_in(seeds[11], 71), 0)
    return dict(queries=queries, response_keys=response_keys, response_values=response_values, output_gradient=output_gradient, prompt_token_keys=prompt_token_keys, prompt_token_values=prompt_token_values, normed_hidden_input=normed_hidden_input, adapter_down_factor=adapter_down_factor, adapter_up_factor=adapter_up_factor, response_prompt_index=response_prompt_index, response_lengths=response_lengths)


adapter_scale = 2.0

def respond(query_rows, key_own, value_own, grad_rows, key_prompt, value_prompt, length):
    row_count = query_rows.shape[0]
    kv_heads = key_own.shape[1] // HEAD_SIZE
    query_group_width = QUERY_HEAD_COUNT // KEY_VALUE_HEADS
    prompt_count = key_prompt.shape[0]
    key_count = prompt_count + row_count
    score_scale = 1.0 / math.sqrt(HEAD_SIZE)
    query_heads = query_rows.reshape(row_count, kv_heads, query_group_width, HEAD_SIZE).astype(jnp.float32)
    keys_all = jnp.concatenate([key_prompt, key_own], 0).reshape(key_count, kv_heads, HEAD_SIZE).astype(jnp.float32)
    values_all = jnp.concatenate([value_prompt, value_own], 0).reshape(key_count, kv_heads, HEAD_SIZE).astype(jnp.float32)
    scores = jnp.einsum('lgcd,mgd->gclm', query_heads, keys_all) * score_scale
    column = jnp.arange(key_count, dtype=jnp.int32)[None, :]
    position = jnp.arange(row_count, dtype=jnp.int32)[:, None]
    own_index = column - prompt_count
    visible = (column < prompt_count) | (own_index <= position) & (own_index < length)
    denominator = lax.optimization_barrier(jnp.sum(jnp.where(visible, jnp.exp(scores), 0.0), axis=-1, keepdims=True))
    log_total = jnp.log(denominator)
    weights = jnp.where(visible, jnp.exp(scores - log_total), 0.0)
    weights_low = weights.astype(jnp.bfloat16).astype(jnp.float32)
    live = (jnp.arange(row_count, dtype=jnp.int32) < length)[:, None, None, None]
    grad_heads = grad_rows.reshape(row_count, kv_heads, query_group_width, HEAD_SIZE)
    grad_live = jnp.where(live, grad_heads, jnp.zeros_like(grad_heads)).astype(jnp.float32)
    output = jnp.einsum('gclm,mgd->lgcd', weights_low, values_all)
    row_dot = lax.optimization_barrier(jnp.sum(grad_live * output, axis=-1))
    weight_grad = jnp.einsum('lgcd,mgd->gclm', grad_live, values_all)
    score_grad = (weights * (weight_grad - jnp.transpose(row_dot, (1, 2, 0))[..., None])).astype(jnp.bfloat16).astype(jnp.float32)
    query_part = jnp.einsum('gclm,mgd->lgcd', score_grad, keys_all) * score_scale
    key_part = jnp.einsum('gclm,lgcd->mgd', score_grad, query_heads) * score_scale
    value_part = jnp.einsum('gclm,lgcd->mgd', weights_low, grad_live)
    return (query_part.reshape(row_count, -1).astype(jnp.bfloat16), key_part[prompt_count:].reshape(row_count, -1).astype(jnp.bfloat16), value_part[prompt_count:].reshape(row_count, -1).astype(jnp.bfloat16), key_part[:prompt_count].reshape(prompt_count, -1), value_part[:prompt_count].reshape(prompt_count, -1))

def reference(queries, response_keys, response_values, output_gradient, prompt_token_keys, prompt_token_values, normed_hidden_input, adapter_down_factor, adapter_up_factor, response_prompt_index, response_lengths):

    def one_response(items):
        query_rows, key_own, value_own, grad_rows, owner, length = items
        key_prompt = lax.dynamic_index_in_dim(prompt_token_keys, owner, 0, keepdims=False)
        value_prompt = lax.dynamic_index_in_dim(prompt_token_values, owner, 0, keepdims=False)
        return respond(query_rows, key_own, value_own, grad_rows, key_prompt, value_prompt, length)

    def device_turn(carry, device):
        key_total, value_total = carry
        begin = (device * GROUP).astype(jnp.int32)

        def take_rows(array):
            return lax.dynamic_slice_in_dim(array, begin, GROUP, 0)
        owners_here = take_rows(response_prompt_index)
        results = lax.map(one_response, (take_rows(queries), take_rows(response_keys), take_rows(response_values), take_rows(output_gradient), owners_here, take_rows(response_lengths)))
        query_part, key_own_grad, value_own_grad, key_parts, value_parts = results
        owner_table = (jnp.arange(PROMPT_COUNT, dtype=jnp.int32)[:, None] == owners_here[None, :]).astype(jnp.float32)
        key_share = jnp.einsum('nr,rpk->npk', owner_table, key_parts, precision=lax.Precision.HIGHEST)
        value_share = jnp.einsum('nr,rpk->npk', owner_table, value_parts, precision=lax.Precision.HIGHEST)
        key_low = lax.optimization_barrier(key_share.astype(jnp.bfloat16))
        value_low = lax.optimization_barrier(value_share.astype(jnp.bfloat16))
        key_total = key_total + key_low.astype(jnp.float32)
        value_total = value_total + value_low.astype(jnp.float32)
        return ((key_total, value_total), (query_part, key_own_grad, value_own_grad))
    blank_array = jnp.zeros((PROMPT_COUNT, PROMPT_LENGTH, KEY_VALUE_HEADS * HEAD_SIZE), jnp.float32)
    totals, stacked_rows = lax.scan(device_turn, (blank_array, blank_array), jnp.arange(N_DP, dtype=jnp.int32))
    query_grad = stacked_rows[0].reshape(RESPONSE_COUNT, RESPONSE_LENGTH, QUERY_HEAD_COUNT * HEAD_SIZE)
    response_key_gradient = stacked_rows[1].reshape(RESPONSE_COUNT, RESPONSE_LENGTH, KEY_VALUE_HEADS * HEAD_SIZE)
    response_value_gradient = stacked_rows[2].reshape(RESPONSE_COUNT, RESPONSE_LENGTH, KEY_VALUE_HEADS * HEAD_SIZE)
    prompt_key_grad = totals[0].astype(jnp.bfloat16)
    prompt_value_grad = totals[1].astype(jnp.bfloat16)
    flattened_hidden = normed_hidden_input.reshape(TOTAL_TOKENS, MODEL_WIDTH)
    flattened_gradient = query_grad.reshape(TOTAL_TOKENS, QUERY_HEAD_COUNT * HEAD_SIZE)
    inner_lowrank = jnp.dot(flattened_hidden, adapter_down_factor, preferred_element_type=jnp.float32).astype(jnp.bfloat16)
    backward_lowrank = jnp.dot(flattened_gradient, adapter_up_factor.T, preferred_element_type=jnp.float32).astype(jnp.bfloat16)
    adapter_product = adapter_scale / math.sqrt(TOTAL_TOKENS)
    down_factor_gradient = jnp.dot(flattened_hidden.T, backward_lowrank, preferred_element_type=jnp.float32) * adapter_product
    up_factor_gradient = jnp.dot(inner_lowrank.T, flattened_gradient, preferred_element_type=jnp.float32) * adapter_product
    return (query_grad, response_key_gradient, response_value_gradient, prompt_key_grad, prompt_value_grad, down_factor_gradient, up_factor_gradient)
```

```python
import functools
import math

import jax
import jax.numpy as jnp
import numpy as np
from jax import lax
from jax.experimental import pallas as pl
from jax.experimental.pallas import tpu as pltpu
from jax.sharding import PartitionSpec as P

QUERY_HEAD_COUNT = 64
KEY_VALUE_HEADS = 8
HEAD_SIZE = 128
QUERY_GROUP = QUERY_HEAD_COUNT // KEY_VALUE_HEADS
ROW_STEP = 16
CUTS = 2

adapter_scale = 2.0
MESH = pl.DeviceIdType.MESH
F32 = jnp.float32
BF16 = jnp.bfloat16
NT = (((1,), (1,)), ((), ()))


def ring_place(index, n):
    odd = index % 2
    return (1 - odd) * (index // 2) + odd * (n - 1 - index // 2)


def ring_member(place, n):
    place = (place + 2 * n) % n
    upper = place // (n // 2)
    return (1 - upper) * (2 * place) + upper * (2 * (n - 1 - place) + 1)


def enter(dp_peers, mp_peers):
    barrier = pltpu.get_barrier_semaphore()
    for peer in dp_peers:
        pl.semaphore_signal(barrier, inc=1, device_id={"dp": peer}, device_id_type=MESH)
    for peer in mp_peers:
        pl.semaphore_signal(barrier, inc=1, device_id={"mp": peer}, device_id_type=MESH)
    pl.semaphore_wait(barrier, len(dp_peers) + len(mp_peers))


def remote(source, target, send, recv, peer):
    return pltpu.make_async_remote_copy(
        src_ref=source, dst_ref=target, send_sem=send, recv_sem=recv,
        device_id=peer, device_id_type=MESH,
    )


def gather_kernel(
    n, m, pk, pv, hidden, down, gk, gv, inner,
    pieces, ksend, krecv, vsend, vrecv, msend, mrecv,
):
    me = lax.axis_index("dp")
    mine = lax.axis_index("mp")
    place = ring_place(me, n)
    right, left = ring_member(place + 1, n), ring_member(place + n - 1, n)
    mp_peers = [lax.rem(mine + d, m) for d in range(1, m)]
    enter([right, left], mp_peers)

    rows = pk.shape[0] // CUTS
    tokens = hidden.shape[0]
    piece_count = max(1, min(5, tokens // 256))
    piece = tokens // piece_count
    down_rows = down[...]
    kcopies, vcopies, mcopies = [], [], []

    def inner_piece(j):
        span = pl.ds(j * piece, piece)
        pieces[mine, :, span] = lax.dot_general(
            down_rows, hidden[span, :], NT, preferred_element_type=F32
        ).astype(BF16)

    def exchange():
        for d, peer in enumerate(mp_peers):
            copy = remote(
                pieces.at[mine], pieces.at[mine], msend.at[d], mrecv.at[d], {"mp": peer}
            )
            copy.start()
            mcopies.append(copy)

    done = 0
    for step in range(n - 1):
        kowner = ring_member(place + n - step, n)
        vowner = ring_member(place + step, n)
        krow, vrow = [], []
        for cut in range(CUTS):
            span = pl.ds(cut * rows, rows)
            for owner, own, whole, send, recv, to, row, before in (
                (kowner, pk, gk, ksend, krecv, right, krow, kcopies),
                (vowner, pv, gv, vsend, vrecv, left, vrow, vcopies),
            ):
                if step:
                    before[-1][cut].wait_recv()
                copy = remote(
                    own.at[span] if step == 0 else whole.at[owner, span],
                    whole.at[owner, span],
                    send.at[step, cut], recv.at[step, cut], {"dp": to},
                )
                copy.start()
                row.append(copy)
        kcopies.append(krow)
        vcopies.append(vrow)
        if step == 0:
            gk[me] = pk[...]
            gv[me] = pv[...]
        if done < piece_count:
            inner_piece(done)
            done += 1
            if done == piece_count:
                exchange()
    for copy in kcopies[-1] + vcopies[-1]:
        copy.wait_recv()
    for copy in mcopies:
        copy.wait_recv()
    total = pieces[0].astype(F32)
    for j in range(1, m):
        total = total + pieces[j].astype(F32)
    inner[...] = total.astype(BF16)
    for row in kcopies + vcopies + [mcopies]:
        for copy in row:
            copy.wait_send()


def gather(n, m, pk, pv, hidden, down_rows):
    rank = down_rows.shape[0]
    tokens = hidden.shape[0]
    vmem = pl.BlockSpec(memory_space=pltpu.VMEM)
    return pl.pallas_call(
        functools.partial(gather_kernel, n, m),
        out_shape=(
            jax.ShapeDtypeStruct((n,) + pk.shape, BF16),
            jax.ShapeDtypeStruct((n,) + pv.shape, BF16),
            jax.ShapeDtypeStruct((rank, tokens), BF16),
        ),
        in_specs=[vmem] * 4,
        out_specs=(vmem,) * 3,
        scratch_shapes=[
            pltpu.VMEM((m, rank, tokens), BF16),
            pltpu.SemaphoreType.DMA((n - 1, CUTS)),
            pltpu.SemaphoreType.DMA((n - 1, CUTS)),
            pltpu.SemaphoreType.DMA((n - 1, CUTS)),
            pltpu.SemaphoreType.DMA((n - 1, CUTS)),
            pltpu.SemaphoreType.DMA((m - 1,)),
            pltpu.SemaphoreType.DMA((m - 1,)),
        ],
        compiler_params=pltpu.CompilerParams(
            collective_id=0, has_side_effects=True, vmem_limit_bytes=56 * 2**20
        ),
        name="gather_prompts",
    )(pk, pv, hidden, down_rows)


def attention_kernel(
    owners, lengths, q, g, ko, vo, gk, gv, places,
    dq, dko, dvo, kb, vb, kacc, vacc,
):
    r = pl.program_id(0)
    prompt = owners[r]
    length = lengths[r]
    slots = q.shape[1]
    prompt_rows = gk.shape[1]
    kv_heads = gk.shape[2] // HEAD_SIZE
    score_scale = 1.0 / math.sqrt(HEAD_SIZE)

    @pl.when(r == 0)
    def _():
        kacc[...] = jnp.zeros_like(kacc)
        vacc[...] = jnp.zeros_like(vacc)

    def part(count):
        alive = (lax.broadcasted_iota(jnp.int32, (count, HEAD_SIZE), 0) < length)
        alive = alive.astype(F32).astype(BF16)
        width = QUERY_GROUP * count
        place = places[count // ROW_STEP - 1, 0:1, 0:width]
        own_row = lax.broadcasted_iota(jnp.int32, (count, width), 0)
        visible = (own_row <= place) & (own_row < length)
        if count < slots:
            dq[0, count:, :] = jnp.zeros((slots - count, dq.shape[2]), BF16)
            dko[0, count:, :] = jnp.zeros((slots - count, dko.shape[2]), BF16)
            dvo[0, count:, :] = jnp.zeros((slots - count, dvo.shape[2]), BF16)
        for head in range(kv_heads):
            lanes = slice(head * HEAD_SIZE, (head + 1) * HEAD_SIZE)
            first = head * QUERY_GROUP

            def columns(h):
                return slice((first + h) * HEAD_SIZE, (first + h + 1) * HEAD_SIZE)

            queries = jnp.concatenate(
                [q[0, :count, columns(h)] for h in range(QUERY_GROUP)], axis=0
            )
            grads = jnp.concatenate(
                [g[0, :count, columns(h)] * alive for h in range(QUERY_GROUP)], axis=0
            )
            keys = jnp.concatenate([gk[prompt, :, lanes], ko[0, :count, lanes]], axis=0)
            values = jnp.concatenate([gv[prompt, :, lanes], vo[0, :count, lanes]], axis=0)
            scores = lax.dot_general(keys, queries, NT, preferred_element_type=F32)
            powers = jnp.exp2(scores * (score_scale * math.log2(math.e)))
            powers = jnp.concatenate(
                [powers[:prompt_rows], jnp.where(visible, powers[prompt_rows:], 0.0)], axis=0
            )
            inverse = 1.0 / jnp.sum(powers, axis=0, keepdims=True)
            weight_grad = lax.dot_general(values, grads, NT, preferred_element_type=F32)
            weights = powers * inverse
            row_dot = jnp.sum(weights * weight_grad, axis=0, keepdims=True)
            low = weights.astype(BF16)
            score_grad = (weights * (weight_grad - row_dot)).astype(BF16)
            turned = jnp.dot(keys.T, score_grad, preferred_element_type=F32) * score_scale
            query_part = turned.T.astype(BF16)
            for h in range(QUERY_GROUP):
                dq[0, :count, columns(h)] = query_part[h * count : (h + 1) * count]
            key_part = jnp.dot(score_grad, queries, preferred_element_type=F32) * score_scale
            value_part = jnp.dot(low, grads, preferred_element_type=F32)
            kacc[prompt, :, lanes] += key_part[:prompt_rows]
            vacc[prompt, :, lanes] += value_part[:prompt_rows]
            dko[0, :count, lanes] = key_part[prompt_rows:].astype(BF16)
            dvo[0, :count, lanes] = value_part[prompt_rows:].astype(BF16)

    steps = slots // ROW_STEP
    level = (length + (ROW_STEP - 1)) // ROW_STEP
    for k in range(1, steps + 1):
        pl.when(level == k)(functools.partial(part, k * ROW_STEP))

    @pl.when(r == pl.num_programs(0) - 1)
    def _():
        kb[...] = kacc[...].astype(BF16)
        vb[...] = vacc[...].astype(BF16)


def attention(owners, lengths, q, g, ko, vo, gk, gv):
    count, slots, width = q.shape
    own_width = ko.shape[2]
    steps = slots // ROW_STEP
    table = np.zeros((steps, 8, QUERY_GROUP * slots), np.int32)
    for k in range(1, steps + 1):
        used = QUERY_GROUP * k * ROW_STEP
        table[k - 1, :, :used] = np.arange(used, dtype=np.int32) % (k * ROW_STEP)

    def each(last):
        return pl.BlockSpec((1, slots, last), lambda r, *_: (r, 0, 0))

    def whole(shape):
        return pl.BlockSpec(
            shape, lambda r, *_: (0,) * len(shape), pipeline_mode=pl.Buffered(1)
        )

    def whole_out(shape):
        return pl.BlockSpec(shape, lambda r, *_: (0,) * len(shape))

    return pl.pallas_call(
        attention_kernel,
        grid_spec=pltpu.PrefetchScalarGridSpec(
            num_scalar_prefetch=2,
            grid=(count,),
            in_specs=[
                each(width), each(width), each(own_width), each(own_width),
                whole(gk.shape), whole(gv.shape), whole(table.shape),
            ],
            out_specs=[
                each(width), each(own_width), each(own_width),
                whole_out(gk.shape), whole_out(gv.shape),
            ],
            scratch_shapes=[pltpu.VMEM(gk.shape, F32), pltpu.VMEM(gv.shape, F32)],
        ),
        out_shape=(
            jax.ShapeDtypeStruct(q.shape, BF16),
            jax.ShapeDtypeStruct(ko.shape, BF16),
            jax.ShapeDtypeStruct(vo.shape, BF16),
            jax.ShapeDtypeStruct(gk.shape, BF16),
            jax.ShapeDtypeStruct(gv.shape, BF16),
        ),
        compiler_params=pltpu.CompilerParams(vmem_limit_bytes=60 * 2**20),
        name="attention_backward",
    )(owners, lengths, q, g, ko, vo, gk, gv, jnp.asarray(table))


def reduce_kernel(
    n, m, product, kb, vb, inner, up, hidden_far, dq_far,
    pk_out, pv_out, down_out, up_out,
    hidden, dq, kslots, vslots, pieces, terms, shares, final,
    ksend, krecv, vsend, vrecv, msend, mrecv, rsend, rrecv, fsend, frecv, lsem,
):
    me = lax.axis_index("dp")
    mine = lax.axis_index("mp")
    place = ring_place(me, n)
    right, left = ring_member(place + 1, n), ring_member(place + n - 1, n)
    dp_peers = [lax.rem(me + d, n) for d in range(1, n)]
    mp_peers = [lax.rem(mine + d, m) for d in range(1, m)]
    dq_copy = pltpu.make_async_copy(dq_far, dq, lsem.at[0])
    dq_copy.start()
    hidden_copy = pltpu.make_async_copy(hidden_far, hidden, lsem.at[1])
    hidden_copy.start()
    enter(dp_peers, mp_peers)

    rows = kb.shape[1] // CUTS
    lane_blocks = terms.shape[2] // 128
    down_blocks = hidden.shape[1] // 128
    up_blocks = dq.shape[1] // 128
    kcopies, vcopies, mcopies, rcopies, fcopies = [], [], [], [], []

    def ring(step):
        krow, vrow = [], []
        for cut in range(CUTS):
            span = pl.ds(cut * rows, rows)
            for owner, own, slot, send, recv, to, row, before in (
                (ring_member(place + n - 1 - step, n), kb, kslots, ksend, krecv, right, krow, kcopies),
                (ring_member(place + 1 + step, n), vb, vslots, vsend, vrecv, left, vrow, vcopies),
            ):
                if step:
                    before[-1][cut].wait_recv()
                    slot[step - 1, span] = (
                        slot[step - 1, span].astype(F32) + own[owner, span].astype(F32)
                    ).astype(BF16)
                copy = remote(
                    own.at[owner, span] if step == 0 else slot.at[step - 1, span],
                    slot.at[step, span],
                    send.at[step, cut], recv.at[step, cut], {"dp": to},
                )
                copy.start()
                row.append(copy)
        kcopies.append(krow)
        vcopies.append(vrow)

    def back():
        dq_copy.wait()
        pieces[mine] = lax.dot_general(
            up[...], dq[...], NT, preferred_element_type=F32
        ).astype(BF16)
        for d, peer in enumerate(mp_peers):
            copy = remote(
                pieces.at[mine], pieces.at[mine], msend.at[d], mrecv.at[d], {"mp": peer}
            )
            copy.start()
            mcopies.append(copy)

    def put(block, values):
        at = block % lane_blocks * 128
        terms[block // lane_blocks, :, at : at + 128] = values

    def up_term():
        term = jnp.dot(inner[...], dq[...], preferred_element_type=F32) * product
        term = term.astype(BF16)
        for b in range(up_blocks):
            put(down_blocks + b, term[:, b * 128 : (b + 1) * 128])
        for b in range(down_blocks + up_blocks, n * lane_blocks):
            put(b, jnp.zeros((terms.shape[1], 128), BF16))

    def down_term():
        hidden_copy.wait()
        for copy in mcopies:
            copy.wait_recv()
        total = pieces[0].astype(F32)
        for j in range(1, m):
            total = total + pieces[j].astype(F32)
        term = jnp.dot(total.astype(BF16), hidden[...], preferred_element_type=F32) * product
        term = term.astype(BF16)
        for b in range(down_blocks):
            put(b, term[:, b * 128 : (b + 1) * 128])
        for d, peer in enumerate(dp_peers):
            copy = remote(
                terms.at[peer], shares.at[me], rsend.at[d], rrecv.at[d], {"dp": peer}
            )
            copy.start()
            rcopies.append(copy)
        shares[me] = terms[me]

    def sum_terms():
        for copy in rcopies:
            copy.wait_recv()
        total = shares[0].astype(F32)
        for j in range(1, n):
            total = total + shares[j].astype(F32)
        final[me] = total.astype(BF16)
        for d, peer in enumerate(dp_peers):
            copy = remote(
                final.at[me], final.at[me], fsend.at[d], frecv.at[d], {"dp": peer}
            )
            copy.start()
            fcopies.append(copy)

    todo = {0: [back], 1: [up_term], 2: [down_term], 4: [sum_terms]}
    for step in range(n - 1):
        ring(step)
        for action in todo.get(step, ()):
            action()
    for cut in range(CUTS):
        span = pl.ds(cut * rows, rows)
        for own, slot, out, last in (
            (kb, kslots, pk_out, kcopies[-1]), (vb, vslots, pv_out, vcopies[-1]),
        ):
            last[cut].wait_recv()
            out[span] = (
                slot[n - 2, span].astype(F32) + own[me, span].astype(F32)
            ).astype(BF16)
    for copy in fcopies:
        copy.wait_recv()
    for b in range(down_blocks + up_blocks):
        at = b % lane_blocks * 128
        block = final[b // lane_blocks, :, at : at + 128].astype(F32)
        if b < down_blocks:
            down_out[:, b * 128 : (b + 1) * 128] = block
        else:
            up_out[:, (b - down_blocks) * 128 : (b - down_blocks + 1) * 128] = block
    for row in kcopies + vcopies + [mcopies, rcopies, fcopies]:
        for copy in row:
            copy.wait_send()


def reduce(n, m, product, kb, vb, inner, up, hidden, dq):
    rank = up.shape[0]
    tokens, depth = hidden.shape
    width = dq.shape[1]
    lanes = -(-(depth + width) // (128 * n)) * 128
    vmem = pl.BlockSpec(memory_space=pltpu.VMEM)
    far = pl.BlockSpec(memory_space=pl.ANY)
    block = kb.shape[1:]
    dma = pltpu.SemaphoreType.DMA
    return pl.pallas_call(
        functools.partial(reduce_kernel, n, m, product),
        out_shape=(
            jax.ShapeDtypeStruct(block, BF16),
            jax.ShapeDtypeStruct(block, BF16),
            jax.ShapeDtypeStruct((rank, depth), F32),
            jax.ShapeDtypeStruct((rank, width), F32),
        ),
        in_specs=[vmem] * 4 + [far] * 2,
        out_specs=(vmem,) * 4,
        scratch_shapes=[
            pltpu.VMEM((tokens, depth), BF16),
            pltpu.VMEM((tokens, width), BF16),
            pltpu.VMEM((n - 1,) + block, BF16),
            pltpu.VMEM((n - 1,) + block, BF16),
            pltpu.VMEM((m, rank, tokens), BF16),
            pltpu.VMEM((n, rank, lanes), BF16),
            pltpu.VMEM((n, rank, lanes), BF16),
            pltpu.VMEM((n, rank, lanes), BF16),
            dma((n - 1, CUTS)), dma((n - 1, CUTS)), dma((n - 1, CUTS)), dma((n - 1, CUTS)),
            dma((m - 1,)), dma((m - 1,)),
            dma((n - 1,)), dma((n - 1,)), dma((n - 1,)), dma((n - 1,)),
            dma((2,)),
        ],
        compiler_params=pltpu.CompilerParams(
            collective_id=1, has_side_effects=True, vmem_limit_bytes=56 * 2**20
        ),
        name="reduce_gradients",
    )(kb, vb, inner, up, hidden, dq)


def shards(
    queries,
    response_keys,
    response_values,
    output_gradient,
    prompt_token_keys,
    prompt_token_values,
    normed_hidden_input,
    adapter_down_factor,
    adapter_up_factor,
    response_prompt_index,
    response_lengths,
):
    n, m = lax.axis_size("dp"), lax.axis_size("mp")
    hidden = normed_hidden_input.reshape(-1, normed_hidden_input.shape[2])
    gk, gv, inner = gather(
        n, m, prompt_token_keys[0], prompt_token_values[0], hidden, adapter_down_factor.T
    )
    dq, dko, dvo, kb, vb = attention(
        response_prompt_index, response_lengths, queries, output_gradient,
        response_keys, response_values, gk, gv,
    )
    product = adapter_scale / math.sqrt(hidden.shape[0] * n)
    pk, pv, down, up = reduce(
        n, m, product, kb, vb, inner, adapter_up_factor, hidden,
        dq.reshape(-1, dq.shape[2]),
    )
    return dq, dko, dvo, pk[None], pv[None], down.T, up


def solution(mesh):
    rows = P("dp", None, "mp")
    placed = (rows,) * 7 + (P("mp", None), P(None, "mp"), P("dp"), P("dp"))
    return jax.shard_map(
        shards,
        mesh=mesh,
        in_specs=placed,
        out_specs=(rows,) * 5 + (P("mp", None), P(None, "mp")),
        check_vma=False,
    )
```

```python
import functools
import math

import jax
import jax.numpy as jnp
import numpy as np
from jax import lax
from jax.experimental import pallas as pl
from jax.experimental.pallas import tpu as pltpu
from jax.sharding import PartitionSpec as P

QUERY_HEAD_COUNT = 64
KEY_VALUE_HEADS = 8
HEAD_SIZE = 128
QUERY_GROUP = QUERY_HEAD_COUNT // KEY_VALUE_HEADS
ROW_STEP = 16
CUTS = 2

adapter_scale = 2.0
MESH = pl.DeviceIdType.MESH
F32 = jnp.float32
BF16 = jnp.bfloat16
NT = (((1,), (1,)), ((), ()))


def ring_place(index, n):
    odd = index % 2
    return (1 - odd) * (index // 2) + odd * (n - 1 - index // 2)


def ring_member(place, n):
    place = (place + 2 * n) % n
    upper = place // (n // 2)
    return (1 - upper) * (2 * place) + upper * (2 * (n - 1 - place) + 1)


def enter(dp_peers, mp_peers):
    barrier = pltpu.get_barrier_semaphore()
    for peer in dp_peers:
        pl.semaphore_signal(barrier, inc=1, device_id={"dp": peer}, device_id_type=MESH)
    for peer in mp_peers:
        pl.semaphore_signal(barrier, inc=1, device_id={"mp": peer}, device_id_type=MESH)
    pl.semaphore_wait(barrier, len(dp_peers) + len(mp_peers))


def remote(source, target, send, recv, peer):
    return pltpu.make_async_remote_copy(
        src_ref=source, dst_ref=target, send_sem=send, recv_sem=recv,
        device_id=peer, device_id_type=MESH,
    )


def gather_kernel(
    n, m, pk, pv, hidden_far, down, gk, gv, inner,
    hidden, pieces, ksend, krecv, vsend, vrecv, msend, mrecv, lsem,
):
    me = lax.axis_index("dp")
    mine = lax.axis_index("mp")
    place = ring_place(me, n)
    right, left = ring_member(place + 1, n), ring_member(place + n - 1, n)
    mp_peers = [lax.rem(mine + d, m) for d in range(1, m)]
    hidden_copy = pltpu.make_async_copy(hidden_far, hidden, lsem.at[0])
    hidden_copy.start()
    enter([right, left], mp_peers)

    rows = pk.shape[0] // CUTS
    tokens = hidden.shape[0]
    piece_count = max(1, min(5, tokens // 256))
    piece = tokens // piece_count
    down_rows = down[...]
    kcopies, vcopies, mcopies = [], [], []

    def inner_piece(j):
        span = pl.ds(j * piece, piece)
        pieces[mine, :, span] = lax.dot_general(
            down_rows, hidden[span, :], NT, preferred_element_type=F32
        ).astype(BF16)

    def exchange():
        for d, peer in enumerate(mp_peers):
            copy = remote(
                pieces.at[mine], pieces.at[mine], msend.at[d], mrecv.at[d], {"mp": peer}
            )
            copy.start()
            mcopies.append(copy)

    done = 0
    for step in range(n - 1):
        kowner = ring_member(place + n - step, n)
        vowner = ring_member(place + step, n)
        krow, vrow = [], []
        for cut in range(CUTS):
            span = pl.ds(cut * rows, rows)
            for owner, own, whole, send, recv, to, row, before in (
                (kowner, pk, gk, ksend, krecv, right, krow, kcopies),
                (vowner, pv, gv, vsend, vrecv, left, vrow, vcopies),
            ):
                if step:
                    before[-1][cut].wait_recv()
                copy = remote(
                    own.at[span] if step == 0 else whole.at[owner, span],
                    whole.at[owner, span],
                    send.at[step, cut], recv.at[step, cut], {"dp": to},
                )
                copy.start()
                row.append(copy)
        kcopies.append(krow)
        vcopies.append(vrow)
        if step == 0:
            gk[me] = pk[...]
            gv[me] = pv[...]
            hidden_copy.wait()
        if done < piece_count:
            inner_piece(done)
            done += 1
            if done == piece_count:
                exchange()
    for copy in mcopies:
        copy.wait_recv()
    total = pieces[0].astype(F32)
    for j in range(1, m):
        total = total + pieces[j].astype(F32)
    inner[...] = total.astype(BF16)
    for copy in kcopies[-1] + vcopies[-1]:
        copy.wait_recv()
    for row in kcopies + vcopies + [mcopies]:
        for copy in row:
            copy.wait_send()


def gather(n, m, pk, pv, hidden, down_rows):
    rank = down_rows.shape[0]
    tokens = hidden.shape[0]
    vmem = pl.BlockSpec(memory_space=pltpu.VMEM)
    return pl.pallas_call(
        functools.partial(gather_kernel, n, m),
        out_shape=(
            jax.ShapeDtypeStruct((n,) + pk.shape, BF16),
            jax.ShapeDtypeStruct((n,) + pv.shape, BF16),
            jax.ShapeDtypeStruct((rank, tokens), BF16),
        ),
        in_specs=[vmem, vmem, pl.BlockSpec(memory_space=pl.ANY), vmem],
        out_specs=(vmem,) * 3,
        scratch_shapes=[
            pltpu.VMEM(hidden.shape, BF16),
            pltpu.VMEM((m, rank, tokens), BF16),
            pltpu.SemaphoreType.DMA((n - 1, CUTS)),
            pltpu.SemaphoreType.DMA((n - 1, CUTS)),
            pltpu.SemaphoreType.DMA((n - 1, CUTS)),
            pltpu.SemaphoreType.DMA((n - 1, CUTS)),
            pltpu.SemaphoreType.DMA((m - 1,)),
            pltpu.SemaphoreType.DMA((m - 1,)),
            pltpu.SemaphoreType.DMA((1,)),
        ],
        compiler_params=pltpu.CompilerParams(
            collective_id=0, has_side_effects=True, vmem_limit_bytes=56 * 2**20
        ),
        name="gather_prompts",
    )(pk, pv, hidden, down_rows)


def attention_kernel(
    owners, lengths, q, g, ko, vo, gk, gv, places,
    dq, dko, dvo, kb, vb, kacc, vacc,
):
    r = pl.program_id(0)
    prompt = owners[r]
    length = lengths[r]
    slots = q.shape[1]
    prompt_rows = gk.shape[1]
    kv_heads = gk.shape[2] // HEAD_SIZE
    score_scale = 1.0 / math.sqrt(HEAD_SIZE)

    @pl.when(r == 0)
    def _():
        kacc[...] = jnp.zeros_like(kacc)
        vacc[...] = jnp.zeros_like(vacc)

    def part(count):
        alive = (lax.broadcasted_iota(jnp.int32, (count, HEAD_SIZE), 0) < length)
        alive = alive.astype(F32).astype(BF16)
        width = QUERY_GROUP * count
        place = places[count // ROW_STEP - 1, 0:1, 0:width]
        own_row = lax.broadcasted_iota(jnp.int32, (count, width), 0)
        visible = (own_row <= place) & (own_row < length)
        if count < slots:
            dq[0, count:, :] = jnp.zeros((slots - count, dq.shape[2]), BF16)
            dko[0, count:, :] = jnp.zeros((slots - count, dko.shape[2]), BF16)
            dvo[0, count:, :] = jnp.zeros((slots - count, dvo.shape[2]), BF16)
        for head in range(kv_heads):
            lanes = slice(head * HEAD_SIZE, (head + 1) * HEAD_SIZE)
            first = head * QUERY_GROUP

            def columns(h):
                return slice((first + h) * HEAD_SIZE, (first + h + 1) * HEAD_SIZE)

            queries = jnp.concatenate(
                [q[0, :count, columns(h)] for h in range(QUERY_GROUP)], axis=0
            )
            grads = jnp.concatenate(
                [g[0, :count, columns(h)] * alive for h in range(QUERY_GROUP)], axis=0
            )
            keys = jnp.concatenate([gk[prompt, :, lanes], ko[0, :count, lanes]], axis=0)
            values = jnp.concatenate([gv[prompt, :, lanes], vo[0, :count, lanes]], axis=0)
            scores = lax.dot_general(keys, queries, NT, preferred_element_type=F32)
            powers = jnp.exp2(scores * (score_scale * math.log2(math.e)))
            powers = jnp.concatenate(
                [powers[:prompt_rows], jnp.where(visible, powers[prompt_rows:], 0.0)], axis=0
            )
            inverse = 1.0 / jnp.sum(powers, axis=0, keepdims=True)
            weight_grad = lax.dot_general(values, grads, NT, preferred_element_type=F32)
            weights = powers * inverse
            row_dot = jnp.sum(weights * weight_grad, axis=0, keepdims=True)
            low = weights.astype(BF16)
            score_grad = (weights * (weight_grad - row_dot)).astype(BF16)
            turned = jnp.dot(keys.T, score_grad, preferred_element_type=F32) * score_scale
            query_part = turned.T.astype(BF16)
            for h in range(QUERY_GROUP):
                dq[0, :count, columns(h)] = query_part[h * count : (h + 1) * count]
            key_part = jnp.dot(score_grad, queries, preferred_element_type=F32) * score_scale
            value_part = jnp.dot(low, grads, preferred_element_type=F32)
            kacc[prompt, :, lanes] += key_part[:prompt_rows]
            vacc[prompt, :, lanes] += value_part[:prompt_rows]
            dko[0, :count, lanes] = key_part[prompt_rows:].astype(BF16)
            dvo[0, :count, lanes] = value_part[prompt_rows:].astype(BF16)

    steps = slots // ROW_STEP
    level = (length + (ROW_STEP - 1)) // ROW_STEP
    for k in range(1, steps + 1):
        pl.when(level == k)(functools.partial(part, k * ROW_STEP))

    @pl.when(r == pl.num_programs(0) - 1)
    def _():
        kb[...] = kacc[...].astype(BF16)
        vb[...] = vacc[...].astype(BF16)


def attention(owners, lengths, q, g, ko, vo, gk, gv):
    count, slots, width = q.shape
    own_width = ko.shape[2]
    steps = slots // ROW_STEP
    table = np.zeros((steps, 8, QUERY_GROUP * slots), np.int32)
    for k in range(1, steps + 1):
        used = QUERY_GROUP * k * ROW_STEP
        table[k - 1, :, :used] = np.arange(used, dtype=np.int32) % (k * ROW_STEP)

    def each(last):
        return pl.BlockSpec((1, slots, last), lambda r, *_: (r, 0, 0))

    def whole(shape):
        return pl.BlockSpec(
            shape, lambda r, *_: (0,) * len(shape), pipeline_mode=pl.Buffered(1)
        )

    def whole_out(shape):
        return pl.BlockSpec(shape, lambda r, *_: (0,) * len(shape))

    return pl.pallas_call(
        attention_kernel,
        grid_spec=pltpu.PrefetchScalarGridSpec(
            num_scalar_prefetch=2,
            grid=(count,),
            in_specs=[
                each(width), each(width), each(own_width), each(own_width),
                whole(gk.shape), whole(gv.shape), whole(table.shape),
            ],
            out_specs=[
                each(width), each(own_width), each(own_width),
                whole_out(gk.shape), whole_out(gv.shape),
            ],
            scratch_shapes=[pltpu.VMEM(gk.shape, F32), pltpu.VMEM(gv.shape, F32)],
        ),
        out_shape=(
            jax.ShapeDtypeStruct(q.shape, BF16),
            jax.ShapeDtypeStruct(ko.shape, BF16),
            jax.ShapeDtypeStruct(vo.shape, BF16),
            jax.ShapeDtypeStruct(gk.shape, BF16),
            jax.ShapeDtypeStruct(gv.shape, BF16),
        ),
        compiler_params=pltpu.CompilerParams(vmem_limit_bytes=60 * 2**20),
        name="attention_backward",
    )(owners, lengths, q, g, ko, vo, gk, gv, jnp.asarray(table))


def reduce_kernel(
    n, m, product, kb, vb, inner, up, hidden_far, dq_far,
    pk_out, pv_out, final,
    hidden, dq, kslots, vslots, pieces, terms, shares,
    ksend, krecv, vsend, vrecv, msend, mrecv, rsend, rrecv, fsend, frecv, lsem,
):
    me = lax.axis_index("dp")
    mine = lax.axis_index("mp")
    place = ring_place(me, n)
    right, left = ring_member(place + 1, n), ring_member(place + n - 1, n)
    dp_peers = [lax.rem(me + d, n) for d in range(1, n)]
    mp_peers = [lax.rem(mine + d, m) for d in range(1, m)]
    dq_copy = pltpu.make_async_copy(dq_far, dq, lsem.at[0])
    dq_copy.start()
    hidden_copy = pltpu.make_async_copy(hidden_far, hidden, lsem.at[1])
    hidden_copy.start()
    enter(dp_peers, mp_peers)

    rows = kb.shape[1] // CUTS
    lane_blocks = terms.shape[2] // 128
    down_blocks = hidden.shape[1] // 128
    up_blocks = dq.shape[1] // 128
    tokens = hidden.shape[0]
    piece_count = max(1, min(5, tokens // 256))
    piece = tokens // piece_count
    kcopies, vcopies, mcopies, rcopies, fcopies = [], [], [], [], []

    def ring(step, cut):
        if cut == 0:
            kcopies.append([])
            vcopies.append([])
        span = pl.ds(cut * rows, rows)
        for owner, own, slot, send, recv, to, copies in (
            (ring_member(place + n - 1 - step, n), kb, kslots, ksend, krecv, right, kcopies),
            (ring_member(place + 1 + step, n), vb, vslots, vsend, vrecv, left, vcopies),
        ):
            if step:
                copies[step - 1][cut].wait_recv()
                slot[step - 1, span] = (
                    slot[step - 1, span].astype(F32) + own[owner, span].astype(F32)
                ).astype(BF16)
            copy = remote(
                own.at[owner, span] if step == 0 else slot.at[step - 1, span],
                slot.at[step, span],
                send.at[step, cut], recv.at[step, cut], {"dp": to},
            )
            copy.start()
            copies[step].append(copy)

    def back(j):
        if j == 0:
            dq_copy.wait()
        span = pl.ds(j * piece, piece)
        pieces[mine, :, span] = lax.dot_general(
            up[...], dq[span, :], NT, preferred_element_type=F32
        ).astype(BF16)

    def send_back():
        for d, peer in enumerate(mp_peers):
            copy = remote(
                pieces.at[mine], pieces.at[mine], msend.at[d], mrecv.at[d], {"mp": peer}
            )
            copy.start()
            mcopies.append(copy)

    def put(block, values):
        at = block % lane_blocks * 128
        terms[block // lane_blocks, :, at : at + 128] = values

    def up_term(j):
        at = j * 256
        term = jnp.dot(inner[...], dq[:, at : at + 256], preferred_element_type=F32) * product
        term = term.astype(BF16)
        for b in range(2):
            put(down_blocks + 2 * j + b, term[:, b * 128 : (b + 1) * 128])

    def down_term(j):
        at = j * 256
        term = jnp.dot(pieces[0], hidden[:, at : at + 256], preferred_element_type=F32) * product
        term = term.astype(BF16)
        for b in range(2):
            put(2 * j + b, term[:, b * 128 : (b + 1) * 128])

    def take_back():
        hidden_copy.wait()
        for copy in mcopies:
            copy.wait_recv()
        for copy in mcopies:
            copy.wait_send()
        total = pieces[0].astype(F32)
        for j in range(1, m):
            total = total + pieces[j].astype(F32)
        pieces[0] = total.astype(BF16)

    def send_terms():
        for b in range(down_blocks + up_blocks, n * lane_blocks):
            put(b, jnp.zeros((terms.shape[1], 128), BF16))
        for d, peer in enumerate(dp_peers):
            copy = remote(
                terms.at[peer], shares.at[me], rsend.at[d], rrecv.at[d], {"dp": peer}
            )
            copy.start()
            rcopies.append(copy)
        shares[me] = terms[me]

    def sum_terms():
        for copy in rcopies:
            copy.wait_recv()
        total = shares[0].astype(F32)
        for j in range(1, n):
            total = total + shares[j].astype(F32)
        final[me] = total.astype(BF16)
        for d, peer in enumerate(dp_peers):
            copy = remote(
                final.at[me], final.at[me], fsend.at[d], frecv.at[d], {"dp": peer}
            )
            copy.start()
            fcopies.append(copy)

    tasks = [functools.partial(back, j) for j in range(piece_count)] + [send_back]
    ups = [functools.partial(up_term, j) for j in range(up_blocks // 2)]
    tasks += ups[: len(ups) // 2] + [take_back]
    tasks += [functools.partial(down_term, j) for j in range(down_blocks // 2)]
    tasks += ups[len(ups) // 2 :] + [send_terms]
    begins = (n - 1) * CUTS * 5 // 7
    after = [[] for _ in range((n - 1) * CUTS)]
    for k, task in enumerate(tasks):
        after[k * begins // len(tasks)].append(task)
    after[(n - 1) * CUTS - CUTS - 1].append(sum_terms)
    for step in range(n - 1):
        for cut in range(CUTS):
            ring(step, cut)
            for task in after[step * CUTS + cut]:
                task()
    for cut in range(CUTS):
        span = pl.ds(cut * rows, rows)
        for own, slot, out, last in (
            (kb, kslots, pk_out, kcopies[-1]), (vb, vslots, pv_out, vcopies[-1]),
        ):
            last[cut].wait_recv()
            out[span] = (
                slot[n - 2, span].astype(F32) + own[me, span].astype(F32)
            ).astype(BF16)
    for copy in fcopies:
        copy.wait_recv()
    for row in kcopies + vcopies + [rcopies, fcopies]:
        for copy in row:
            copy.wait_send()


def reduce(n, m, product, kb, vb, inner, up, hidden, dq):
    rank = up.shape[0]
    tokens, depth = hidden.shape
    width = dq.shape[1]
    lanes = -(-(depth + width) // (128 * n)) * 128
    vmem = pl.BlockSpec(memory_space=pltpu.VMEM)
    far = pl.BlockSpec(memory_space=pl.ANY)
    block = kb.shape[1:]
    dma = pltpu.SemaphoreType.DMA
    return pl.pallas_call(
        functools.partial(reduce_kernel, n, m, product),
        out_shape=(
            jax.ShapeDtypeStruct(block, BF16),
            jax.ShapeDtypeStruct(block, BF16),
            jax.ShapeDtypeStruct((n, rank, lanes), BF16),
        ),
        in_specs=[vmem] * 4 + [far] * 2,
        out_specs=(vmem,) * 3,
        scratch_shapes=[
            pltpu.VMEM((tokens, depth), BF16),
            pltpu.VMEM((tokens, width), BF16),
            pltpu.VMEM((n - 1,) + block, BF16),
            pltpu.VMEM((n - 1,) + block, BF16),
            pltpu.VMEM((m, rank, tokens), BF16),
            pltpu.VMEM((n, rank, lanes), BF16),
            pltpu.VMEM((n, rank, lanes), BF16),
            dma((n - 1, CUTS)), dma((n - 1, CUTS)), dma((n - 1, CUTS)), dma((n - 1, CUTS)),
            dma((m - 1,)), dma((m - 1,)),
            dma((n - 1,)), dma((n - 1,)), dma((n - 1,)), dma((n - 1,)),
            dma((2,)),
        ],
        compiler_params=pltpu.CompilerParams(
            collective_id=1, has_side_effects=True, vmem_limit_bytes=56 * 2**20
        ),
        name="reduce_gradients",
    )(kb, vb, inner, up, hidden, dq)


def place_kernel(pk, pv, terms, pk_out, pv_out, down_out, up_out):
    pk_out[0] = pk[...]
    pv_out[0] = pv[...]
    lane_blocks = terms.shape[2] // 128
    down_blocks = down_out.shape[1] // 128
    for b in range(down_blocks + up_out.shape[1] // 128):
        at = b % lane_blocks * 128
        block = terms[b // lane_blocks, :, at : at + 128].astype(F32)
        if b < down_blocks:
            down_out[:, b * 128 : (b + 1) * 128] = block
        else:
            up_out[:, (b - down_blocks) * 128 : (b - down_blocks + 1) * 128] = block


def place_results(pk, pv, terms, depth, width):
    rank = terms.shape[1]
    vmem = pl.BlockSpec(memory_space=pltpu.VMEM)
    return pl.pallas_call(
        place_kernel,
        out_shape=(
            jax.ShapeDtypeStruct((1,) + pk.shape, BF16),
            jax.ShapeDtypeStruct((1,) + pv.shape, BF16),
            jax.ShapeDtypeStruct((rank, depth), F32),
            jax.ShapeDtypeStruct((rank, width), F32),
        ),
        in_specs=[vmem] * 3,
        out_specs=(vmem,) * 4,
        name="place_results",
    )(pk, pv, terms)


def shards(
    queries,
    response_keys,
    response_values,
    output_gradient,
    prompt_token_keys,
    prompt_token_values,
    normed_hidden_input,
    adapter_down_factor,
    adapter_up_factor,
    response_prompt_index,
    response_lengths,
):
    n, m = lax.axis_size("dp"), lax.axis_size("mp")
    hidden = normed_hidden_input.reshape(-1, normed_hidden_input.shape[2])
    gk, gv, inner = gather(
        n, m, prompt_token_keys[0], prompt_token_values[0], hidden, adapter_down_factor.T
    )
    dq, dko, dvo, kb, vb = attention(
        response_prompt_index, response_lengths, queries, output_gradient,
        response_keys, response_values, gk, gv,
    )
    product = adapter_scale / math.sqrt(hidden.shape[0] * n)
    pk, pv, terms = reduce(
        n, m, product, kb, vb, inner, adapter_up_factor, hidden,
        dq.reshape(-1, dq.shape[2]),
    )
    pk, pv, down, up = place_results(pk, pv, terms, hidden.shape[1], dq.shape[2])
    return dq, dko, dvo, pk, pv, down.T, up


def solution(mesh):
    rows = P("dp", None, "mp")
    placed = (rows,) * 7 + (P("mp", None), P(None, "mp"), P("dp"), P("dp"))
    return jax.shard_map(
        shards,
        mesh=mesh,
        in_specs=placed,
        out_specs=(rows,) * 5 + (P("mp", None), P(None, "mp")),
        check_vma=False,
    )
```
